32 devices in a mesh: dp: 4 (over y, x), expert: 8 (over z, core).
Axes of the slice: x: 2, y: 2, z: 4, core: 2. Of those that a mesh axis runs over, the one named last changes fastest.
Arguments:
- tokens: bfloat16 [4096, 3584], P(('dp', 'expert')), may hold values from -6 to 6
- grad_out: bfloat16 [4096, 3584], P(('dp', 'expert')), may hold values from -1.5 to 1.5
- route: int32 [4, 8, 8, 1], P('dp', 'expert'), may hold values from 0 to 127
- gates: bfloat16 [4, 8, 8, 1], P('dp', 'expert'), may hold values from 0.099609375 to 1
- w_gate: bfloat16 [8, 3584, 768], P('expert', 'dp'), may hold values from -0.09375 to 0.09375
- w_up: bfloat16 [8, 3584, 768], P('expert', 'dp'), may hold values from -0.09375 to 0.09375
- w_down: bfloat16 [8, 768, 3584], P('expert', None, 'dp'), may hold values from -0.21875 to 0.21875
Outputs:
- grad_tokens: bfloat16 [4096, 3584], P(('dp', 'expert'))
- grad_w_gate: bfloat16 [8, 3584, 768], P('expert', 'dp')
- grad_w_up: bfloat16 [8, 3584, 768], P('expert', 'dp')
- grad_w_down: bfloat16 [8, 768, 3584], P('expert', None, 'dp')
- grad_gates: float32 [4, 8, 8, 1], P('dp', 'expert')
The draws below stay inside these ranges and needn't reach their ends.
Inputs may be any that keep to these rules, and one draw needn't show every extreme that they name: route[i, j, e, s] is the position, among the 128 tokens of the device at dp index i and expert index j, of the token that expert e takes in slot s from that device; a token may be taken by several experts or slots.
All inputs are finite; a program needn't handle non-finite values.
Results may differ from the reference program's by a relative error of at most 0.017.
Values may be sent and summed in bfloat16 or wider, within the bound.
No kernel may reach another device: no remote copies, remote signals or barrier semaphores. Data moves between devices by JAX's collectives and lax.ppermute only.
A program may use at most 64 MiB of HBM per device.

```python
import math
import jax
import jax.numpy as jnp
from jax import lax

D = 3584
H = 768
SLOT = 1
TOK_DEV = 128
EXPERTS = 8
TOKENS = 4096
N_DP = 4
N_EXPERT = 8


def touch_ends(values, own_key, low, top_value):
    place = [jax.random.randint(jax.random.fold_in(own_key, axis), (), 0, length) for axis, length in enumerate(values.shape)]
    main_axis = values.shape.index(max(values.shape))
    next_to = place[:main_axis] + [(place[main_axis] + 1) % values.shape[main_axis]] + place[main_axis + 1:]
    return values.at[tuple(place)].set(low).at[tuple(next_to)].set(top_value)


def steps_of(stream_key, shape, cuts, least, top_value):
    def one(position, parts):
        draws = jax.random.uniform(jax.random.fold_in(jax.random.fold_in(stream_key, 6), position), (parts,), jnp.float32, least / len(cuts), top_value / len(cuts))
        return jnp.repeat(jnp.exp(draws), shape[position] // parts).reshape((-1,) + (1,) * (len(shape) - position - 1))

    level = one(*cuts[0])
    for cut in cuts[1:]:
        level = level * one(*cut)
    return level


def gaussian(own_key, dims, width, reach, split=(), kind=jnp.bfloat16):
    values = jax.random.normal(own_key, dims, jnp.float32) * width
    if len(split) > 0:
        values = steps_of(own_key, dims, split, -0.22, 0.18) * values
    return jnp.clip(values, min=-reach, max=reach).astype(kind)


def setup_inputs(seed: int = 0) -> dict:
    arg_keys = jax.random.split(jax.random.key(seed), 8)
    return {
        "tokens": gaussian(arg_keys[0], (TOKENS, D), 1.0, 6.0, ((0, 32),)),
        "grad_out": gaussian(arg_keys[1], (TOKENS, D), 0.25, 1.5, ((0, 32),)),
        "route": touch_ends(jax.random.randint(arg_keys[2], (N_DP, N_EXPERT, EXPERTS, SLOT), 0, TOK_DEV), jax.random.fold_in(arg_keys[2], 1), 0, TOK_DEV - 1).astype(jnp.int32),
        "gates": jnp.clip(jnp.exp(math.log(1.0) - 2.306499 * jax.random.uniform(arg_keys[3], (N_DP, N_EXPERT, EXPERTS, SLOT), jnp.float32) ** steps_of(arg_keys[3], (N_DP, N_EXPERT, EXPERTS, SLOT), ((0, 4), (1, 8)), -0.2, 0.2)), 0.099609375, 1.0).astype(jnp.bfloat16),
        "w_gate": gaussian(arg_keys[4], (EXPERTS, D, H), D ** -0.5, 0.09375, ((0, 8), (1, 4))),
        "w_up": gaussian(arg_keys[5], (EXPERTS, D, H), D ** -0.5, 0.09375, ((0, 8), (1, 4))),
        "w_down": gaussian(arg_keys[6], (EXPERTS, H, D), H ** -0.5, 0.21875, ((0, 8), (2, 4))),
    }


def reference(tokens, grad_out, route, gates, w_gate, w_up, w_down):
    n_dp, n_ex, experts, slots = route.shape
    rows = n_dp * n_ex * slots
    offsets = (jnp.arange(n_dp * n_ex, dtype=jnp.int32) * TOK_DEV).reshape(n_dp, n_ex, 1, 1)
    chosen = jnp.transpose(route + offsets, (2, 0, 1, 3)).reshape(experts, rows).astype(jnp.int32)
    weights_of = jnp.transpose(gates, (2, 0, 1, 3)).reshape(experts, rows)

    def one_expert(args):
        picks, gate_w, wg, wu, wd = args
        x_rows = tokens[picks]
        dy_rows = grad_out[picks]
        gate_pre = jnp.dot(x_rows, wg, preferred_element_type=jnp.float32)
        up_pre = jnp.dot(x_rows, wu, preferred_element_type=jnp.float32)
        hidden = (jax.nn.silu(gate_pre) * up_pre).astype(jnp.bfloat16)
        out_rows = jnp.dot(hidden, wd, preferred_element_type=jnp.float32).astype(jnp.bfloat16)
        grad_gate = jnp.sum(dy_rows.astype(jnp.float32) * out_rows.astype(jnp.float32), axis=1)
        weighted = (gate_w.astype(jnp.float32)[:, None] * dy_rows.astype(jnp.float32)).astype(jnp.bfloat16)
        grad_hidden = jnp.dot(weighted, wd.T, preferred_element_type=jnp.float32)
        sig = jax.nn.sigmoid(gate_pre)
        grad_gate_pre = (grad_hidden * up_pre * sig * (1.0 + gate_pre * (1.0 - sig))).astype(jnp.bfloat16)
        grad_up_pre = (grad_hidden * gate_pre * sig).astype(jnp.bfloat16)
        grad_rows = (jnp.dot(grad_gate_pre, wg.T, preferred_element_type=jnp.float32)
                     + jnp.dot(grad_up_pre, wu.T, preferred_element_type=jnp.float32)).astype(jnp.bfloat16)
        grad_wg = jnp.dot(x_rows.T, grad_gate_pre, preferred_element_type=jnp.float32).astype(jnp.bfloat16)
        grad_wu = jnp.dot(x_rows.T, grad_up_pre, preferred_element_type=jnp.float32).astype(jnp.bfloat16)
        grad_wd = jnp.dot(hidden.T, weighted, preferred_element_type=jnp.float32).astype(jnp.bfloat16)
        return grad_gate, grad_rows, grad_wg, grad_wu, grad_wd

    grad_gate, grad_rows, grad_wg, grad_wu, grad_wd = lax.map(
        one_expert, (chosen, weights_of, w_gate, w_up, w_down))
    grad_tokens = jnp.zeros((TOKENS, D), jnp.float32).at[chosen.reshape(-1)].add(
        grad_rows.reshape(experts * rows, D).astype(jnp.float32)).astype(jnp.bfloat16)
    grad_gates = jnp.transpose(grad_gate.reshape(experts, n_dp, n_ex, slots), (1, 2, 0, 3))
    return grad_tokens, grad_wg, grad_wu, grad_wd, grad_gates
```

```python
import functools

import jax
import jax.numpy as jnp
from jax import lax
from jax.experimental import pallas as pl
from jax.experimental.pallas import tpu as pltpu
from jax.sharding import PartitionSpec as P

LANES = 128
F32 = jnp.float32
BF16 = jnp.bfloat16
AXES = ("dp", "expert")


def dot(left, right, left_dim=1, right_dim=0):
    return lax.dot_general(
        left, right, (((left_dim,), (right_dim,)), ((), ())), preferred_element_type=F32
    )


def call(body, outs, scratch=()):
    return pl.pallas_call(
        body,
        out_shape=[jax.ShapeDtypeStruct(shape, kind) for shape, kind in outs],
        scratch_shapes=[pltpu.VMEM(shape, kind) for shape, kind in scratch],
        compiler_params=pltpu.CompilerParams(vmem_limit_bytes=40 << 20),
    )


def pick_matrix(route, tokens):
    places = lax.broadcasted_iota(jnp.int32, (route.shape[0], tokens), 1)
    return (places == route).astype(F32).astype(BF16)


def pack_kernel(n_dp, lines, depth, route, gates, tokens, grad_out, message, scratch):
    experts = route.shape[0]
    chunks = tokens.shape[1] // LANES // n_dp
    pick = pick_matrix(route[...], tokens.shape[0])
    scratch[...] = jnp.zeros_like(scratch)
    for source, first in ((tokens, 0), (grad_out, chunks)):
        rows = dot(pick, source[...])
        for i in range(n_dp):
            for k in range(chunks):
                lane = (i * chunks + k) * LANES
                start = i * experts * depth + first + k
                scratch[pl.ds(start, experts, stride=depth), :] = rows[:, lane:lane + LANES]
    gate = jnp.broadcast_to(gates[...].astype(F32), (experts, LANES))
    for i in range(n_dp):
        scratch[pl.ds(i * experts * depth + 2 * chunks, experts, stride=depth), :] = gate
    message[...] = scratch[...].astype(BF16).reshape(message.shape)


def partial_kernel(depth, message, wg, wu, wd, part, x_rows, weighted, gate_col, scratch):
    rows = message.shape[0]
    hidden = wg.shape[1]
    chunks = wg.shape[0] // LANES
    scratch[...] = message[...].astype(F32).reshape(scratch.shape)
    gate = scratch[pl.ds(2 * chunks, rows, stride=depth), :]
    gate_col[...] = gate
    xs, dys = [], []
    for k in range(chunks):
        xs.append(scratch[pl.ds(k, rows, stride=depth), :].astype(BF16))
        dy = scratch[pl.ds(chunks + k, rows, stride=depth), :]
        dys.append(dy.astype(BF16))
        weighted[:, k * LANES:(k + 1) * LANES] = (gate * dy).astype(BF16)
    x = jnp.concatenate(xs, axis=1)
    dy = jnp.concatenate(dys, axis=1)
    x_rows[...] = x
    part[:, :hidden] = dot(x, wg[...]).astype(BF16)
    part[:, hidden:2 * hidden] = dot(x, wu[...]).astype(BF16)
    part[:, 2 * hidden:] = dot(dy, wd[...], 1, 1).astype(BF16)


def middle_kernel(depth, mine, other, gate_col, wg, wu, back, hidden_out, ggp_out, gup_out, scratch):
    rows = mine.shape[0]
    hidden = wg.shape[1]
    chunks = wg.shape[0] // LANES
    pre = mine[...].astype(F32) + other[...].astype(F32)
    gate_pre = pre[:, :hidden]
    up_pre = pre[:, hidden:2 * hidden]
    grad_plain = pre[:, 2 * hidden:]
    sig = 1.0 / (1.0 + jnp.exp(-gate_pre))
    silu = gate_pre * sig
    act = (silu * up_pre).astype(BF16)
    grad = grad_plain * gate_col[:, :1]
    ggp = (grad * up_pre * sig * (1.0 + gate_pre * (1.0 - sig))).astype(BF16)
    gup = (grad * silu).astype(BF16)
    hidden_out[...] = act
    ggp_out[...] = ggp
    gup_out[...] = gup
    result = dot(ggp, wg[...], 1, 1) + dot(gup, wu[...], 1, 1)
    for k in range(chunks):
        scratch[pl.ds(k, rows, stride=depth), :] = result[:, k * LANES:(k + 1) * LANES]
    value = jnp.sum(act.astype(F32) * grad_plain, axis=1, keepdims=True)
    high = value.astype(BF16).astype(F32)
    mid = (value - high).astype(BF16).astype(F32)
    low = value - high - mid
    lane = lax.broadcasted_iota(jnp.int32, (rows, LANES), 1)
    pieces = jnp.where(lane == 0, high, jnp.where(lane == 1, mid, jnp.where(lane == 2, low, 0.0)))
    for k in range(chunks, depth):
        scratch[pl.ds(k, rows, stride=depth), :] = pieces
    back[...] = scratch[...].astype(BF16).reshape(back.shape)


def weights_kernel(x_rows, weighted, act, ggp, gup, grad_wg, grad_wu, grad_wd):
    grad_wg[0] = dot(x_rows[...], ggp[...], 0, 0).astype(BF16)
    grad_wu[0] = dot(x_rows[...], gup[...], 0, 0).astype(BF16)
    grad_wd[0] = dot(act[...], weighted[...], 0, 0).astype(BF16)


def unpack_kernel(n_dp, depth, chunks, route, back, grad_tokens, grad_gates, scratch):
    experts = route.shape[0]
    scratch[...] = back[...].astype(F32).reshape(scratch.shape)
    pick = pick_matrix(route[...], grad_tokens.shape[0])
    for i in range(n_dp):
        first = i * experts * depth
        rows = [
            scratch[pl.ds(first + k, experts, stride=depth), :].astype(BF16)
            for k in range(chunks)
        ]
        lane = i * chunks * LANES
        grad_tokens[:, lane:lane + chunks * LANES] = dot(
            pick, jnp.concatenate(rows, axis=1), 0, 0
        ).astype(BF16)
    pieces = scratch[pl.ds(chunks, experts, stride=depth), :]
    grad_gates[...] = jnp.broadcast_to(
        jnp.sum(pieces, axis=1, keepdims=True), grad_gates.shape
    )


def sum_over_dp(part):
    n_dp = lax.axis_size("dp")
    n_ex = lax.axis_size("expert")
    bits = n_dp.bit_length() - 1
    mine = part
    other = None
    for step in range(bits):
        if other is not None:
            mine = (mine.astype(F32) + other.astype(F32)).astype(BF16)
        pairs = []
        for i in range(n_dp):
            for e in range(n_ex):
                partner = i ^ (1 << ((step + e) % bits))
                pairs.append((i * n_ex + e, partner * n_ex + e))
        other = lax.ppermute(mine, AXES, pairs)
    return mine, other


def local_tiled(tokens, grad_out, route, gates, w_gate, w_up, w_down):
    n_dp = lax.axis_size("dp")
    n_ex = lax.axis_size("expert")
    experts = route.shape[2]
    n_tok, width = tokens.shape
    piece = width // n_dp
    hidden = w_gate.shape[2]
    chunks = piece // LANES
    devices = n_dp * n_ex
    depth = -(-(2 * chunks + 1) // 16) * 16
    back_depth = -(-(chunks + 1) // 8) * 8
    wg, wu, wd = w_gate[0], w_up[0], w_down[0]
    picks = route.reshape(experts, 1)
    gate_in = gates.reshape(experts, 1)

    (message,) = call(
        functools.partial(pack_kernel, n_dp, chunks, depth),
        [((devices, depth, LANES), BF16)],
        [((devices * depth, LANES), F32)],
    )(picks, gate_in, tokens, grad_out)
    arrived = lax.all_to_all(message, AXES, 0, 0, tiled=True)
    part, x_rows, weighted, gate_col = call(
        functools.partial(partial_kernel, depth),
        [
            ((devices, 3 * hidden), BF16),
            ((devices, piece), BF16),
            ((devices, piece), BF16),
            ((devices, LANES), F32),
        ],
        [((devices * depth, LANES), F32)],
    )(arrived, wg, wu, wd)
    mine, other = sum_over_dp(part)
    back, act, ggp, gup = call(
        functools.partial(middle_kernel, back_depth),
        [
            ((devices, back_depth, LANES), BF16),
            ((devices, hidden), BF16),
            ((devices, hidden), BF16),
            ((devices, hidden), BF16),
        ],
        [((devices * back_depth, LANES), F32)],
    )(mine, other, gate_col, wg, wu)
    returned = lax.all_to_all(back, AXES, 0, 0, tiled=True)
    grad_wg, grad_wu, grad_wd = call(
        weights_kernel,
        [(w_gate.shape, BF16), (w_up.shape, BF16), (w_down.shape, BF16)],
    )(x_rows, weighted, act, ggp, gup)
    grad_tokens, grad_gates = call(
        functools.partial(unpack_kernel, n_dp, back_depth, chunks),
        [((n_tok, width), BF16), ((experts, LANES), F32)],
        [((devices * back_depth, LANES), F32)],
    )(picks, returned)
    return grad_tokens, grad_wg, grad_wu, grad_wd, grad_gates[:, 0].reshape(gates.shape)


def local_plain(tokens, grad_out, route, gates, w_gate, w_up, w_down):
    n_dp = lax.axis_size("dp")
    n_ex = lax.axis_size("expert")
    experts, slots = route.shape[2:]
    n_tok, width = tokens.shape
    piece = width // n_dp
    hidden = w_gate.shape[2]
    rows = n_dp * n_ex * slots
    wg, wu, wd = w_gate[0], w_up[0], w_down[0]
    picks = route.reshape(experts * slots)

    def runs(source):
        picked = jnp.take(source, picks, axis=0).reshape(experts, slots, n_dp, piece)
        return picked.transpose(2, 0, 1, 3).reshape(n_dp * experts, slots, piece)

    gate_cols = jnp.broadcast_to(
        gates.reshape(1, experts, slots, 1), (n_dp, experts, slots, 1)
    ).reshape(n_dp * experts, slots, 1)
    message = jnp.concatenate([runs(tokens), runs(grad_out), gate_cols], axis=2)
    arrived = lax.all_to_all(message, AXES, 0, 0, tiled=True).reshape(rows, 2 * piece + 1)
    x_rows, dy_rows = arrived[:, :piece], arrived[:, piece:2 * piece]
    gate = arrived[:, 2 * piece:].astype(F32)
    weighted = (gate * dy_rows.astype(F32)).astype(BF16)
    part = jnp.concatenate(
        [dot(x_rows, wg), dot(x_rows, wu), dot(dy_rows, wd, 1, 1)], axis=1
    )
    pre = lax.psum(part, "dp")
    gate_pre, up_pre, grad_plain = jnp.split(pre, 3, axis=1)
    sig = jax.nn.sigmoid(gate_pre)
    silu = gate_pre * sig
    act = (silu * up_pre).astype(BF16)
    grad = grad_plain * gate
    ggp = (grad * up_pre * sig * (1.0 + gate_pre * (1.0 - sig))).astype(BF16)
    gup = (grad * silu).astype(BF16)
    result = (dot(ggp, wg, 1, 1) + dot(gup, wu, 1, 1)).astype(BF16)
    value = jnp.sum(act.astype(F32) * grad_plain, axis=1, keepdims=True)
    high = value.astype(BF16)
    low = (value - high.astype(F32)).astype(BF16)
    back = jnp.concatenate([result, high, low], axis=1).reshape(n_dp * n_ex, slots, piece + 2)
    returned = lax.all_to_all(back, AXES, 0, 0, tiled=True)
    returned = returned.reshape(n_dp, experts * slots, piece + 2)
    flat = returned[:, :, :piece].transpose(1, 0, 2).reshape(experts * slots, width)
    grad_tokens = jnp.zeros((n_tok, width), F32).at[picks].add(flat.astype(F32)).astype(BF16)
    grad_gates = returned[0, :, piece:].astype(F32).sum(axis=1).reshape(gates.shape)
    return (
        grad_tokens,
        dot(x_rows, ggp, 0, 0).astype(BF16)[None],
        dot(x_rows, gup, 0, 0).astype(BF16)[None],
        dot(act, weighted, 0, 0).astype(BF16)[None],
        grad_gates,
    )


def solution(mesh):
    def local(tokens, grad_out, route, gates, w_gate, w_up, w_down):
        n_dp = lax.axis_size("dp")
        tiled = (
            w_gate.shape[1] % LANES == 0
            and route.shape[2] % 8 == 0
            and route.shape[3] == 1
            and n_dp & (n_dp - 1) == 0
            and n_dp > 1
        )
        body = local_tiled if tiled else local_plain
        return body(tokens, grad_out, route, gates, w_gate, w_up, w_down)

    return jax.shard_map(
        local,
        mesh=mesh,
        in_specs=(
            P(("dp", "expert"), None),
            P(("dp", "expert"), None),
            P("dp", "expert", None, None),
            P("dp", "expert", None, None),
            P("expert", "dp", None),
            P("expert", "dp", None),
            P("expert", None, "dp"),
        ),
        out_specs=(
            P(("dp", "expert"), None),
            P("expert", "dp", None),
            P("expert", "dp", None),
            P("expert", None, "dp"),
            P("dp", "expert", None, None),
        ),
        check_vma=False,
    )
```

```python
import functools

import jax
import jax.numpy as jnp
from jax import lax
from jax.experimental import pallas as pl
from jax.experimental.pallas import tpu as pltpu
from jax.sharding import PartitionSpec as P

LANES = 128
F32 = jnp.float32
BF16 = jnp.bfloat16
AXES = ("dp", "expert")


def dot(left, right, left_dim=1, right_dim=0):
    return lax.dot_general(
        left, right, (((left_dim,), (right_dim,)), ((), ())), preferred_element_type=F32
    )


def call(body, outs, scratch=(), in_hbm=(), out_hbm=(), inputs=0, copies=0, limit=24):
    def spec(hbm):
        return pl.BlockSpec(memory_space=pltpu.HBM if hbm else pltpu.VMEM)

    shapes = [pltpu.VMEM(shape, kind) for shape, kind in scratch]
    if copies:
        shapes.append(pltpu.SemaphoreType.DMA((copies,)))
    return pl.pallas_call(
        body,
        out_shape=[jax.ShapeDtypeStruct(shape, kind) for shape, kind in outs],
        in_specs=[spec(k in in_hbm) for k in range(inputs)],
        out_specs=[spec(k in out_hbm) for k in range(len(outs))],
        scratch_shapes=shapes,
        compiler_params=pltpu.CompilerParams(vmem_limit_bytes=limit << 20),
    )


def in_hbm(array):
    return pltpu.with_memory_space_constraint(array, pltpu.HBM)


DP_ORDERS = {4: (0, 1, 3, 2)}
EXPERT_ORDERS = {8: (7, 1, 4, 0, 3, 6, 5, 2)}


def dp_order(n):
    return DP_ORDERS.get(n, tuple(range(n)))


def expert_order(n):
    return EXPERT_ORDERS.get(n, tuple(range(n)))


def match(order):
    n = len(order)
    row = lax.broadcasted_iota(jnp.int32, (n, n), 0)
    column = lax.broadcasted_iota(jnp.int32, (n, n), 1)
    wanted = jnp.zeros((n, n), jnp.int32)
    for k, index in enumerate(order):
        wanted = jnp.where(row == k, index, wanted)
    return column == wanted


def to_column(row, order):
    n = row.shape[1]
    spread = jnp.where(match(order), jnp.broadcast_to(row.astype(F32), (n, n)), 0.0)
    return jnp.sum(spread, axis=1, keepdims=True)


def to_row(column, order):
    n = column.shape[0]
    spread = jnp.where(match(order), jnp.broadcast_to(column, (n, n)), 0.0)
    return jnp.sum(spread, axis=0, keepdims=True)


def first_lines(n_dp, experts, depth):
    return [dp_order(n_dp).index(i) * experts * depth for i in range(n_dp)]


def exchange(blocks):
    n_dp = lax.axis_size("dp")
    n_ex = lax.axis_size("expert")
    order = [i * n_ex + e for i in dp_order(n_dp) for e in expert_order(n_ex)]
    return lax.all_to_all(blocks, AXES, 0, 0, tiled=True, axis_index_groups=[order])


def pack_kernel(
    n_dp, depth, route, gates, tokens, grad_out, w_down, message, wd, picks,
    held, scratch, route_in, gates_in, sems,
):
    experts = route.shape[1]
    width = tokens.shape[1]
    piece = width // n_dp
    chunks = piece // LANES
    targets = (held.at[0], held.at[1], route_in, gates_in, wd)
    copies = [
        pltpu.make_async_copy(source, target, sems.at[s])
        for s, (source, target) in enumerate(zip((tokens, grad_out, route, gates, w_down), targets))
    ]
    for s in (2, 3, 0, 1, 4):
        copies[s].start()
    copies[2].wait()
    copies[3].wait()
    places = lax.broadcasted_iota(jnp.int32, (experts, tokens.shape[0]), 1).astype(F32)
    column = to_column(route_in[...], expert_order(experts))
    picks[...] = (places == column).astype(F32)
    pick = picks[...].astype(BF16)
    gate = jnp.broadcast_to(to_column(gates_in[...], expert_order(experts)), (experts, LANES))
    zero = jnp.zeros((experts, LANES), F32)
    firsts = first_lines(n_dp, experts, depth)
    for first in firsts:
        for k in range(2 * chunks, depth):
            scratch[pl.ds(first + k, experts, stride=depth), :] = gate if k == 2 * chunks else zero
    for s in range(2):
        copies[s].wait()
        rows = dot(pick, held[s])
        for i in range(n_dp):
            for k in range(chunks):
                start = firsts[i] + s * chunks + k
                lane = i * piece + k * LANES
                scratch[pl.ds(start, experts, stride=depth), :] = rows[:, lane:lane + LANES]
    message[...] = scratch[...].astype(BF16).reshape(message.shape)
    copies[4].wait()


def partial_kernel(
    depth, message, wg, w_up, wd, part, x_rows, weighted, gate_col, wu, scratch, sems
):
    rows = message.shape[0]
    _, hidden, piece = wd.shape
    chunks = piece // LANES
    copy = pltpu.make_async_copy(w_up, wu, sems.at[0])
    copy.start()
    scratch[...] = message[...].astype(F32).reshape(scratch.shape)
    gate = scratch[pl.ds(2 * chunks, rows, stride=depth), :]
    gate_col[...] = gate
    xs, dys = [], []
    for k in range(chunks):
        xs.append(scratch[pl.ds(k, rows, stride=depth), :].astype(BF16))
        dy = scratch[pl.ds(chunks + k, rows, stride=depth), :]
        dys.append(dy.astype(BF16))
        weighted[:, k * LANES:(k + 1) * LANES] = (gate * dy).astype(BF16)
    x = jnp.concatenate(xs, axis=1)
    dy = jnp.concatenate(dys, axis=1)
    x_rows[...] = x
    part[:, :hidden] = dot(x, wg[0]).astype(BF16)
    part[:, 2 * hidden:] = dot(dy, wd[0], 1, 1).astype(BF16)
    copy.wait()
    part[:, hidden:2 * hidden] = dot(x, wu[0]).astype(BF16)


def turn_kernel(wg, wu, turned):
    hidden = wg.shape[2]
    for s, source in enumerate((wg, wu)):
        for k in range(hidden // LANES):
            first = s * hidden + k * LANES
            turned[first:first + LANES, :] = source[0, :, k * LANES:(k + 1) * LANES].T


def middle_kernel(depth, count, *refs):
    parts, (gate_col, turned, back, hidden_out, ggp_out, gup_out, scratch) = (
        refs[:count], refs[count:]
    )
    rows = parts[0].shape[0]
    hidden = turned.shape[0] // 2
    chunks = turned.shape[1] // LANES
    terms = [part[...].astype(F32) for part in parts]
    while len(terms) > 1:
        terms = [terms[k] + terms[k + 1] for k in range(0, len(terms), 2)]
    pre = terms[0]
    gate_pre = pre[:, :hidden]
    up_pre = pre[:, hidden:2 * hidden]
    grad_plain = pre[:, 2 * hidden:]
    sig = 1.0 / (1.0 + jnp.exp(-gate_pre))
    silu = gate_pre * sig
    act = (silu * up_pre).astype(BF16)
    grad = grad_plain * gate_col[:, :1]
    ggp = (grad * up_pre * sig * (1.0 + gate_pre * (1.0 - sig))).astype(BF16)
    gup = (grad * silu).astype(BF16)
    hidden_out[...] = act
    ggp_out[...] = ggp
    gup_out[...] = gup
    result = dot(jnp.concatenate([ggp, gup], axis=1), turned[...])
    for k in range(chunks):
        scratch[pl.ds(k, rows, stride=depth), :] = result[:, k * LANES:(k + 1) * LANES]
    value = jnp.sum(act.astype(F32) * grad_plain, axis=1, keepdims=True)
    high = value.astype(BF16).astype(F32)
    mid = (value - high).astype(BF16).astype(F32)
    low = value - high - mid
    lane = lax.broadcasted_iota(jnp.int32, (rows, LANES), 1)
    pieces = jnp.where(lane == 0, high, jnp.where(lane == 1, mid, jnp.where(lane == 2, low, 0.0)))
    for k in range(chunks, depth):
        scratch[pl.ds(k, rows, stride=depth), :] = pieces
    back[...] = scratch[...].astype(BF16).reshape(back.shape)


def weights_kernel(x_rows, weighted, act, ggp, gup, grad_wg, grad_wu, grad_wd):
    grad_wg[0] = dot(x_rows[...], ggp[...], 0, 0).astype(BF16)
    grad_wu[0] = dot(x_rows[...], gup[...], 0, 0).astype(BF16)
    grad_wd[0] = dot(act[...], weighted[...], 0, 0).astype(BF16)


def unpack_kernel(
    n_dp, depth, chunks, picks, back, grad_tokens, grad_gates, scratch, held, gates_held, sems
):
    experts = picks.shape[0]
    piece = chunks * LANES
    firsts = first_lines(n_dp, experts, depth)
    scratch[...] = back[...].astype(F32).reshape(scratch.shape)
    pick = picks[...].astype(BF16)
    column = jnp.sum(scratch[pl.ds(firsts[0] + chunks, experts, stride=depth), :], axis=1, keepdims=True)
    gates_held[...] = to_row(column, expert_order(experts))
    copies = [pltpu.make_async_copy(gates_held, grad_gates, sems.at[n_dp])]
    copies[0].start()
    for i in range(n_dp):
        first = firsts[i]
        rows = [
            scratch[pl.ds(first + k, experts, stride=depth), :].astype(BF16)
            for k in range(chunks)
        ]
        lanes = pl.ds(i * piece, piece)
        held[:, i * piece:(i + 1) * piece] = dot(
            pick, jnp.concatenate(rows, axis=1), 0, 0
        ).astype(BF16)
        copies.append(
            pltpu.make_async_copy(held.at[:, lanes], grad_tokens.at[:, lanes], sems.at[i])
        )
        copies[-1].start()
    for copy in copies:
        copy.wait()


def local_tiled(tokens, grad_out, route, gates, w_gate, w_up, w_down):
    n_dp = lax.axis_size("dp")
    n_ex = lax.axis_size("expert")
    experts = route.shape[2]
    n_tok, width = tokens.shape
    piece = width // n_dp
    hidden = w_gate.shape[2]
    chunks = piece // LANES
    devices = n_dp * n_ex
    depth = -(-(2 * chunks + 1) // 16) * 16
    back_depth = -(-(chunks + 1) // 8) * 8
    picks = route.reshape(1, experts)
    gate_in = gates.reshape(1, experts)

    message, wd, chosen = call(
        functools.partial(pack_kernel, n_dp, depth),
        [((devices, depth, LANES), BF16), (w_down.shape, BF16), ((experts, n_tok), F32)],
        [
            ((2, n_tok, width), BF16),
            ((devices * depth, LANES), F32),
            ((1, experts), jnp.int32),
            ((1, experts), BF16),
        ],
        in_hbm=(0, 1, 2, 3, 4),
        inputs=5,
        copies=5,
    )(*map(in_hbm, (picks, gate_in, tokens, grad_out, w_down)))
    arrived = exchange(message)
    part, x_rows, weighted, gate_col, wu = call(
        functools.partial(partial_kernel, depth),
        [
            ((devices, 3 * hidden), BF16),
            ((devices, piece), BF16),
            ((devices, piece), BF16),
            ((devices, LANES), F32),
            ((1, piece, hidden), BF16),
        ],
        [((devices * depth, LANES), F32)],
        in_hbm=(2,),
        inputs=4,
        copies=1,
    )(arrived, w_gate, in_hbm(w_up), wd)
    parts = {0: part}
    for k in sorted(range(1, n_dp), key=lambda k: (k & -k, k), reverse=True):
        parts[k] = lax.ppermute(part, "dp", [(i, i ^ k) for i in range(n_dp)])
    parts = [parts[k] for k in range(n_dp)]
    (turned,) = call(turn_kernel, [((2 * hidden, piece), BF16)], inputs=2)(w_gate, wu)
    back, act, ggp, gup = call(
        functools.partial(middle_kernel, back_depth, n_dp),
        [
            ((devices, back_depth, LANES), BF16),
            ((devices, hidden), BF16),
            ((devices, hidden), BF16),
            ((devices, hidden), BF16),
        ],
        [((devices * back_depth, LANES), F32)],
        inputs=n_dp + 2,
    )(*parts, gate_col, turned)
    returned = exchange(back)
    grad_wg, grad_wu, grad_wd = call(
        weights_kernel,
        [(w_gate.shape, BF16), (w_up.shape, BF16), (w_down.shape, BF16)],
        inputs=5,
    )(x_rows, weighted, act, ggp, gup)
    grad_tokens, grad_gates = call(
        functools.partial(unpack_kernel, n_dp, back_depth, chunks),
        [((n_tok, width), BF16), ((1, experts), F32)],
        [
            ((devices * back_depth, LANES), F32),
            ((n_tok, width), BF16),
            ((1, experts), F32),
        ],
        out_hbm=(0, 1),
        inputs=2,
        copies=n_dp + 1,
    )(chosen, returned)
    return grad_tokens, grad_wg, grad_wu, grad_wd, grad_gates.reshape(gates.shape)


def local_plain(tokens, grad_out, route, gates, w_gate, w_up, w_down):
    n_dp = lax.axis_size("dp")
    n_ex = lax.axis_size("expert")
    experts, slots = route.shape[2:]
    n_tok, width = tokens.shape
    piece = width // n_dp
    hidden = w_gate.shape[2]
    rows = n_dp * n_ex * slots
    wg, wu, wd = w_gate[0], w_up[0], w_down[0]
    picks = route.reshape(experts * slots)

    def runs(source):
        picked = jnp.take(source, picks, axis=0).reshape(experts, slots, n_dp, piece)
        return picked.transpose(2, 0, 1, 3).reshape(n_dp * experts, slots, piece)

    gate_cols = jnp.broadcast_to(
        gates.reshape(1, experts, slots, 1), (n_dp, experts, slots, 1)
    ).reshape(n_dp * experts, slots, 1)
    message = jnp.concatenate([runs(tokens), runs(grad_out), gate_cols], axis=2)
    arrived = lax.all_to_all(message, AXES, 0, 0, tiled=True).reshape(rows, 2 * piece + 1)
    x_rows, dy_rows = arrived[:, :piece], arrived[:, piece:2 * piece]
    gate = arrived[:, 2 * piece:].astype(F32)
    weighted = (gate * dy_rows.astype(F32)).astype(BF16)
    part = jnp.concatenate(
        [dot(x_rows, wg), dot(x_rows, wu), dot(dy_rows, wd, 1, 1)], axis=1
    )
    pre = lax.psum(part, "dp")
    gate_pre, up_pre, grad_plain = jnp.split(pre, 3, axis=1)
    sig = jax.nn.sigmoid(gate_pre)
    silu = gate_pre * sig
    act = (silu * up_pre).astype(BF16)
    grad = grad_plain * gate
    ggp = (grad * up_pre * sig * (1.0 + gate_pre * (1.0 - sig))).astype(BF16)
    gup = (grad * silu).astype(BF16)
    result = (dot(ggp, wg, 1, 1) + dot(gup, wu, 1, 1)).astype(BF16)
    value = jnp.sum(act.astype(F32) * grad_plain, axis=1, keepdims=True)
    high = value.astype(BF16)
    low = (value - high.astype(F32)).astype(BF16)
    back = jnp.concatenate([result, high, low], axis=1).reshape(n_dp * n_ex, slots, piece + 2)
    returned = lax.all_to_all(back, AXES, 0, 0, tiled=True)
    returned = returned.reshape(n_dp, experts * slots, piece + 2)
    flat = returned[:, :, :piece].transpose(1, 0, 2).reshape(experts * slots, width)
    grad_tokens = jnp.zeros((n_tok, width), F32).at[picks].add(flat.astype(F32)).astype(BF16)
    grad_gates = returned[0, :, piece:].astype(F32).sum(axis=1).reshape(gates.shape)
    return (
        grad_tokens,
        dot(x_rows, ggp, 0, 0).astype(BF16)[None],
        dot(x_rows, gup, 0, 0).astype(BF16)[None],
        dot(act, weighted, 0, 0).astype(BF16)[None],
        grad_gates,
    )


def solution(mesh):
    def local(tokens, grad_out, route, gates, w_gate, w_up, w_down):
        n_dp = lax.axis_size("dp")
        tiled = (
            w_gate.shape[1] % LANES == 0
            and route.shape[2] % 8 == 0
            and route.shape[2] == lax.axis_size("expert")
            and route.shape[3] == 1
            and w_gate.shape[2] % LANES == 0
            and n_dp & (n_dp - 1) == 0
        )
        body = local_tiled if tiled else local_plain
        return body(tokens, grad_out, route, gates, w_gate, w_up, w_down)

    return jax.shard_map(
        local,
        mesh=mesh,
        in_specs=(
            P(("dp", "expert"), None),
            P(("dp", "expert"), None),
            P("dp", "expert", None, None),
            P("dp", "expert", None, None),
            P("expert", "dp", None),
            P("expert", "dp", None),
            P("expert", None, "dp"),
        ),
        out_specs=(
            P(("dp", "expert"), None),
            P("expert", "dp", None),
            P("expert", "dp", None),
            P("expert", None, "dp"),
            P("dp", "expert", None, None),
        ),
        check_vma=False,
    )
```

```python
import functools

import jax
import jax.numpy as jnp
from jax import lax
from jax.experimental import pallas as pl
from jax.experimental.pallas import tpu as pltpu
from jax.sharding import PartitionSpec as P

LANES = 128
F32 = jnp.float32
BF16 = jnp.bfloat16
AXES = ("dp", "expert")


def dot(left, right, left_dim=1, right_dim=0):
    return lax.dot_general(
        left, right, (((left_dim,), (right_dim,)), ((), ())), preferred_element_type=F32
    )


def call(body, outs, scratch=(), in_hbm=(), out_hbm=(), inputs=0, copies=0, limit=24, cost=None):
    def spec(hbm):
        return pl.BlockSpec(memory_space=pltpu.HBM if hbm else pltpu.VMEM)

    shapes = [pltpu.VMEM(shape, kind) for shape, kind in scratch]
    if copies:
        shapes.append(pltpu.SemaphoreType.DMA((copies,)))
    return pl.pallas_call(
        body,
        out_shape=[jax.ShapeDtypeStruct(shape, kind) for shape, kind in outs],
        in_specs=[spec(k in in_hbm) for k in range(inputs)],
        out_specs=[spec(k in out_hbm) for k in range(len(outs))],
        scratch_shapes=shapes,
        cost_estimate=cost,
        compiler_params=pltpu.CompilerParams(vmem_limit_bytes=limit << 20),
    )


def in_hbm(array):
    return pltpu.with_memory_space_constraint(array, pltpu.HBM)


DP_ORDERS = {4: (0, 1, 3, 2)}
EXPERT_ORDERS = {8: (7, 1, 4, 0, 3, 6, 5, 2)}


def dp_order(n):
    return DP_ORDERS.get(n, tuple(range(n)))


def expert_order(n):
    return EXPERT_ORDERS.get(n, tuple(range(n)))


def match(order):
    n = len(order)
    row = lax.broadcasted_iota(jnp.int32, (n, n), 0)
    column = lax.broadcasted_iota(jnp.int32, (n, n), 1)
    wanted = jnp.zeros((n, n), jnp.int32)
    for k, index in enumerate(order):
        wanted = jnp.where(row == k, index, wanted)
    return column == wanted


def to_column(row, order):
    n = row.shape[1]
    spread = jnp.where(match(order), jnp.broadcast_to(row.astype(F32), (n, n)), 0.0)
    return jnp.sum(spread, axis=1, keepdims=True)


def to_row(column, order):
    n = column.shape[0]
    spread = jnp.where(match(order), jnp.broadcast_to(column, (n, n)), 0.0)
    return jnp.sum(spread, axis=0, keepdims=True)


def first_lines(n_dp, experts, depth):
    return [dp_order(n_dp).index(i) * experts * depth for i in range(n_dp)]


def exchange(blocks):
    n_dp = lax.axis_size("dp")
    n_ex = lax.axis_size("expert")
    order = [i * n_ex + e for i in dp_order(n_dp) for e in expert_order(n_ex)]
    return lax.all_to_all(blocks, AXES, 0, 0, tiled=True, axis_index_groups=[order])


def pack_kernel(
    n_dp, depth, route, gates, tokens, grad_out, w_down, message, wd, picks,
    held, scratch, route_in, gates_in, sems,
):
    experts = route.shape[1]
    width = tokens.shape[1]
    piece = width // n_dp
    chunks = piece // LANES
    targets = (held.at[0], held.at[1], route_in, gates_in, wd)
    copies = [
        pltpu.make_async_copy(source, target, sems.at[s])
        for s, (source, target) in enumerate(zip((tokens, grad_out, route, gates, w_down), targets))
    ]
    for s in (2, 3, 0, 1, 4):
        copies[s].start()
    copies[2].wait()
    copies[3].wait()
    places = lax.broadcasted_iota(jnp.int32, (experts, tokens.shape[0]), 1).astype(F32)
    column = to_column(route_in[...], expert_order(experts))
    picks[...] = (places == column).astype(F32)
    pick = picks[...].astype(BF16)
    gate = jnp.broadcast_to(to_column(gates_in[...], expert_order(experts)), (experts, LANES))
    zero = jnp.zeros((experts, LANES), F32)
    firsts = first_lines(n_dp, experts, depth)
    for first in firsts:
        for k in range(2 * chunks, depth):
            scratch[pl.ds(first + k, experts, stride=depth), :] = gate if k == 2 * chunks else zero
    for s in range(2):
        copies[s].wait()
        rows = dot(pick, held[s])
        for i in range(n_dp):
            for k in range(chunks):
                start = firsts[i] + s * chunks + k
                lane = i * piece + k * LANES
                scratch[pl.ds(start, experts, stride=depth), :] = rows[:, lane:lane + LANES]
    message[...] = scratch[...].astype(BF16).reshape(message.shape)
    copies[4].wait()


def partial_kernel(depth, message, wg, wd, part, x_rows, weighted, gate_col, scratch):
    rows = message.shape[0]
    _, hidden, piece = wd.shape
    chunks = piece // LANES
    scratch[...] = message[...].astype(F32).reshape(scratch.shape)
    gate = scratch[pl.ds(2 * chunks, rows, stride=depth), :]
    gate_col[...] = gate
    xs, dys = [], []
    for k in range(chunks):
        xs.append(scratch[pl.ds(k, rows, stride=depth), :].astype(BF16))
        dy = scratch[pl.ds(chunks + k, rows, stride=depth), :]
        dys.append(dy.astype(BF16))
        weighted[:, k * LANES:(k + 1) * LANES] = (gate * dy).astype(BF16)
    x = jnp.concatenate(xs, axis=1)
    dy = jnp.concatenate(dys, axis=1)
    x_rows[...] = x
    part[:, :hidden] = dot(x, wg[0]).astype(BF16)
    part[:, hidden:] = dot(dy, wd[0], 1, 1).astype(BF16)


def up_kernel(x_rows, wu, part):
    part[...] = dot(x_rows[...], wu[0]).astype(BF16)


def turn_kernel(wg, wu, turned):
    hidden = wg.shape[2]
    for s, source in enumerate((wg, wu)):
        for k in range(hidden // LANES):
            first = s * hidden + k * LANES
            turned[first:first + LANES, :] = source[0, :, k * LANES:(k + 1) * LANES].T


def sum_kernel(*refs):
    terms = [ref[...].astype(F32) for ref in refs[:-1]]
    while len(terms) > 1:
        terms = [terms[k] + terms[k + 1] for k in range(0, len(terms), 2)]
    refs[-1][...] = terms[0]


def middle_kernel(
    depth, up, mine, other, gate_col, turned, back, hidden_out, ggp_out, gup_out, scratch
):
    rows = gate_col.shape[0]
    hidden = turned.shape[0] // 2
    chunks = turned.shape[1] // LANES
    up_pre = up[...]
    rest = mine[...].astype(F32) + other[...].astype(F32)
    gate_pre = rest[:, :hidden]
    grad_plain = rest[:, hidden:]
    sig = 1.0 / (1.0 + jnp.exp(-gate_pre))
    silu = gate_pre * sig
    act = (silu * up_pre).astype(BF16)
    grad = grad_plain * gate_col[:, :1]
    ggp = (grad * up_pre * sig * (1.0 + gate_pre * (1.0 - sig))).astype(BF16)
    gup = (grad * silu).astype(BF16)
    hidden_out[...] = act
    ggp_out[...] = ggp
    gup_out[...] = gup
    result = dot(jnp.concatenate([ggp, gup], axis=1), turned[...])
    for k in range(chunks):
        scratch[pl.ds(k, rows, stride=depth), :] = result[:, k * LANES:(k + 1) * LANES]
    value = jnp.sum(act.astype(F32) * grad_plain, axis=1, keepdims=True)
    high = value.astype(BF16).astype(F32)
    mid = (value - high).astype(BF16).astype(F32)
    low = value - high - mid
    lane = lax.broadcasted_iota(jnp.int32, (rows, LANES), 1)
    pieces = jnp.where(lane == 0, high, jnp.where(lane == 1, mid, jnp.where(lane == 2, low, 0.0)))
    for k in range(chunks, depth):
        scratch[pl.ds(k, rows, stride=depth), :] = pieces
    back[...] = scratch[...].astype(BF16).reshape(back.shape)


def weights_kernel(x_rows, weighted, act, ggp, gup, grad_wg, grad_wu, grad_wd):
    grad_wg[0] = dot(x_rows[...], ggp[...], 0, 0).astype(BF16)
    grad_wu[0] = dot(x_rows[...], gup[...], 0, 0).astype(BF16)
    grad_wd[0] = dot(act[...], weighted[...], 0, 0).astype(BF16)


def unpack_kernel(
    n_dp, depth, chunks, picks, back, grad_tokens, grad_gates, scratch, held, gates_held, sems
):
    experts = picks.shape[0]
    piece = chunks * LANES
    firsts = first_lines(n_dp, experts, depth)
    scratch[...] = back[...].astype(F32).reshape(scratch.shape)
    pick = picks[...].astype(BF16)
    column = jnp.sum(scratch[pl.ds(firsts[0] + chunks, experts, stride=depth), :], axis=1, keepdims=True)
    gates_held[...] = to_row(column, expert_order(experts))
    copies = [pltpu.make_async_copy(gates_held, grad_gates, sems.at[n_dp])]
    copies[0].start()
    for i in range(n_dp):
        first = firsts[i]
        rows = [
            scratch[pl.ds(first + k, experts, stride=depth), :].astype(BF16)
            for k in range(chunks)
        ]
        lanes = pl.ds(i * piece, piece)
        held[:, i * piece:(i + 1) * piece] = dot(
            pick, jnp.concatenate(rows, axis=1), 0, 0
        ).astype(BF16)
        copies.append(
            pltpu.make_async_copy(held.at[:, lanes], grad_tokens.at[:, lanes], sems.at[i])
        )
        copies[-1].start()
    for copy in copies:
        copy.wait()


def dp_terms(paired, direct):
    n_dp = lax.axis_size("dp")
    n_ex = lax.axis_size("expert")
    bits = n_dp.bit_length() - 1

    def swap(array, masks):
        return lax.ppermute(
            array,
            AXES,
            [
                (i * n_ex + e, (i ^ masks[e % 2]) * n_ex + e)
                for i in range(n_dp)
                for e in range(n_ex)
            ],
        )

    def mask(step, core):
        return 1 << ((step + core) % bits)

    other = swap(paired, (mask(0, 0), mask(0, 1)))
    masks = [(mask(k, 0), mask(k, 1)) for k in range(bits)]
    masks += [(k, k) for k in range(1, n_dp) if k & (k - 1)]
    direct_all = [direct] + [swap(direct, pair) for pair in masks]
    for step in range(1, bits):
        paired = (paired.astype(F32) + other.astype(F32)).astype(BF16)
        other = swap(paired, (mask(step, 0), mask(step, 1)))
    return (paired, other), direct_all


def local_tiled(tokens, grad_out, route, gates, w_gate, w_up, w_down):
    n_dp = lax.axis_size("dp")
    n_ex = lax.axis_size("expert")
    experts = route.shape[2]
    n_tok, width = tokens.shape
    piece = width // n_dp
    hidden = w_gate.shape[2]
    chunks = piece // LANES
    devices = n_dp * n_ex
    depth = -(-(2 * chunks + 1) // 16) * 16
    back_depth = -(-(chunks + 1) // 8) * 8
    picks = route.reshape(1, experts)
    gate_in = gates.reshape(1, experts)

    message, wd, chosen = call(
        functools.partial(pack_kernel, n_dp, depth),
        [((devices, depth, LANES), BF16), (w_down.shape, BF16), ((experts, n_tok), F32)],
        [
            ((2, n_tok, width), BF16),
            ((devices * depth, LANES), F32),
            ((1, experts), jnp.int32),
            ((1, experts), BF16),
        ],
        in_hbm=(0, 1, 2, 3, 4),
        inputs=5,
        copies=5,
    )(*map(in_hbm, (picks, gate_in, tokens, grad_out, w_down)))
    arrived = exchange(message)
    part, x_rows, weighted, gate_col = call(
        functools.partial(partial_kernel, depth),
        [
            ((devices, 2 * hidden), BF16),
            ((devices, piece), BF16),
            ((devices, piece), BF16),
            ((devices, LANES), F32),
        ],
        [((devices * depth, LANES), F32)],
        inputs=3,
    )(arrived, w_gate, wd)
    (up_part,) = call(
        up_kernel,
        [((devices, hidden), BF16)],
        inputs=2,
        cost=pl.CostEstimate(flops=3 * 10**8, bytes_accessed=0, transcendentals=0),
    )(x_rows, w_up)
    (mine, other), direct = dp_terms(part, up_part)
    (up_pre,) = call(
        sum_kernel,
        [((devices, hidden), F32)],
        inputs=n_dp,
        cost=pl.CostEstimate(flops=10**9, bytes_accessed=0, transcendentals=0),
    )(*direct)
    (turned,) = call(turn_kernel, [((2 * hidden, piece), BF16)], inputs=2)(w_gate, w_up)
    back, act, ggp, gup = call(
        functools.partial(middle_kernel, back_depth),
        [
            ((devices, back_depth, LANES), BF16),
            ((devices, hidden), BF16),
            ((devices, hidden), BF16),
            ((devices, hidden), BF16),
        ],
        [((devices * back_depth, LANES), F32)],
        inputs=5,
    )(up_pre, mine, other, gate_col, turned)
    returned = exchange(back)
    grad_wg, grad_wu, grad_wd = call(
        weights_kernel,
        [(w_gate.shape, BF16), (w_up.shape, BF16), (w_down.shape, BF16)],
        inputs=5,
    )(x_rows, weighted, act, ggp, gup)
    grad_tokens, grad_gates = call(
        functools.partial(unpack_kernel, n_dp, back_depth, chunks),
        [((n_tok, width), BF16), ((1, experts), F32)],
        [
            ((devices * back_depth, LANES), F32),
            ((n_tok, width), BF16),
            ((1, experts), F32),
        ],
        out_hbm=(0, 1),
        inputs=2,
        copies=n_dp + 1,
    )(chosen, returned)
    return grad_tokens, grad_wg, grad_wu, grad_wd, grad_gates.reshape(gates.shape)


def local_plain(tokens, grad_out, route, gates, w_gate, w_up, w_down):
    n_dp = lax.axis_size("dp")
    n_ex = lax.axis_size("expert")
    experts, slots = route.shape[2:]
    n_tok, width = tokens.shape
    piece = width // n_dp
    hidden = w_gate.shape[2]
    rows = n_dp * n_ex * slots
    wg, wu, wd = w_gate[0], w_up[0], w_down[0]
    picks = route.reshape(experts * slots)

    def runs(source):
        picked = jnp.take(source, picks, axis=0).reshape(experts, slots, n_dp, piece)
        return picked.transpose(2, 0, 1, 3).reshape(n_dp * experts, slots, piece)

    gate_cols = jnp.broadcast_to(
        gates.reshape(1, experts, slots, 1), (n_dp, experts, slots, 1)
    ).reshape(n_dp * experts, slots, 1)
    message = jnp.concatenate([runs(tokens), runs(grad_out), gate_cols], axis=2)
    arrived = lax.all_to_all(message, AXES, 0, 0, tiled=True).reshape(rows, 2 * piece + 1)
    x_rows, dy_rows = arrived[:, :piece], arrived[:, piece:2 * piece]
    gate = arrived[:, 2 * piece:].astype(F32)
    weighted = (gate * dy_rows.astype(F32)).astype(BF16)
    part = jnp.concatenate(
        [dot(x_rows, wg), dot(x_rows, wu), dot(dy_rows, wd, 1, 1)], axis=1
    )
    pre = lax.psum(part, "dp")
    gate_pre, up_pre, grad_plain = jnp.split(pre, 3, axis=1)
    sig = jax.nn.sigmoid(gate_pre)
    silu = gate_pre * sig
    act = (silu * up_pre).astype(BF16)
    grad = grad_plain * gate
    ggp = (grad * up_pre * sig * (1.0 + gate_pre * (1.0 - sig))).astype(BF16)
    gup = (grad * silu).astype(BF16)
    result = (dot(ggp, wg, 1, 1) + dot(gup, wu, 1, 1)).astype(BF16)
    value = jnp.sum(act.astype(F32) * grad_plain, axis=1, keepdims=True)
    high = value.astype(BF16)
    low = (value - high.astype(F32)).astype(BF16)
    back = jnp.concatenate([result, high, low], axis=1).reshape(n_dp * n_ex, slots, piece + 2)
    returned = lax.all_to_all(back, AXES, 0, 0, tiled=True)
    returned = returned.reshape(n_dp, experts * slots, piece + 2)
    flat = returned[:, :, :piece].transpose(1, 0, 2).reshape(experts * slots, width)
    grad_tokens = jnp.zeros((n_tok, width), F32).at[picks].add(flat.astype(F32)).astype(BF16)
    grad_gates = returned[0, :, piece:].astype(F32).sum(axis=1).reshape(gates.shape)
    return (
        grad_tokens,
        dot(x_rows, ggp, 0, 0).astype(BF16)[None],
        dot(x_rows, gup, 0, 0).astype(BF16)[None],
        dot(act, weighted, 0, 0).astype(BF16)[None],
        grad_gates,
    )


def solution(mesh):
    def local(tokens, grad_out, route, gates, w_gate, w_up, w_down):
        n_dp = lax.axis_size("dp")
        tiled = (
            w_gate.shape[1] % LANES == 0
            and route.shape[2] % 8 == 0
            and route.shape[2] == lax.axis_size("expert")
            and route.shape[3] == 1
            and w_gate.shape[2] % LANES == 0
            and n_dp & (n_dp - 1) == 0
        )
        body = local_tiled if tiled else local_plain
        return body(tokens, grad_out, route, gates, w_gate, w_up, w_down)

    return jax.shard_map(
        local,
        mesh=mesh,
        in_specs=(
            P(("dp", "expert"), None),
            P(("dp", "expert"), None),
            P("dp", "expert", None, None),
            P("dp", "expert", None, None),
            P("expert", "dp", None),
            P("expert", "dp", None),
            P("expert", None, "dp"),
        ),
        out_specs=(
            P(("dp", "expert"), None),
            P("expert", "dp", None),
            P("expert", "dp", None),
            P("expert", None, "dp"),
            P("dp", "expert", None, None),
        ),
        check_vma=False,
    )
```
